768 devices in a mesh: dp: 64 (over x, y, core), table: 12 (over z).
Axes of the slice: x: 4, y: 8, z: 12, core: 2. Of those that a mesh axis runs over, the one named last changes fastest.
Arguments:
- dense_input: bfloat16 [98304, 13], P(('dp', 'table')), may hold values from -6 to 6
- hot_ids: int32 [98304, 52], P(('dp', 'table')), may hold values from 0 to 3071
- logit_grad: float32 [98304], P(('dp', 'table')), may hold values from -0.875 to 0.875
- hot_table: bfloat16 [3072, 128], replicated, may hold values from -6 to 6
- hot_accum: float32 [3072], replicated, may hold values from 0.03 to 1
- cold_table: bfloat16 [393216, 128], P(('dp', 'table')), may hold values from -6 to 6
- cold_accum: float32 [393216], P(('dp', 'table')), may hold values from 3.90625e-06 to 0.00013020834
- send_rows: int32 [9216, 256], P(('dp', 'table')), may hold values from 0 to 511
- send_count: int32 [768, 12], P(('dp', 'table')), may hold values from 1 to 256, as said below
- recv_bags: int32 [9216, 256], P(('dp', 'table')), may hold values from 0 to 3327
- bottom_one: bfloat16 [13, 512], replicated, may hold values from -1.75 to 1.75
- bottom_two: bfloat16 [512, 256], replicated, may hold values from -0.25 to 0.25
- bottom_three: bfloat16 [256, 128], replicated, may hold values from -0.375 to 0.375
- cross_down: bfloat16 [3456, 512], replicated, may hold values from -0.109375 to 0.109375
- cross_up: bfloat16 [512, 3456], replicated, may hold values from -0.25 to 0.25
- head_vector: float32 [3456], replicated, may hold values from -0.109375 to 0.109375
Outputs:
- logits: float32 [98304], P(('dp', 'table'))
- new_hot: float32 [3072, 128], replicated
- new_cold: float32 [393216, 128], P(('dp', 'table'))
The draws below stay inside these ranges and needn't reach their ends.
Inputs may be any that keep to these rules, and one draw needn't show every extreme that they name: `send_count`: live slots of an owner to one sample owner; in every draw some owner fills all 256 slots to some sample owner, and owners' loads differ by up to four times.
All inputs are finite; a program needn't handle non-finite values.
Results may differ from the reference program's by a relative error of at most 0.0046.
Values may be sent and summed in bfloat16 or wider, within the bound.
No kernel may reach another device: no remote copies, remote signals or barrier semaphores. Data moves between devices by JAX's collectives and lax.ppermute only.
A program may use at most 64 MiB of HBM per device.

```python
import math
import jax
import jax.numpy as jnp
import numpy as np
from jax import lax

E = 128
TABLES = 26
DENSE_IN = 13
BOT1 = 512
BOT2 = 256
R = 512
LH = 2
B_DEV = 128
ROWS_DEV = 512
CAP = 256
HOT = 3072
F = 3456
BATCH = 98304
COLD = 393216
N_DP = 64
N_TABLE = 12


def draw_send_count(key, part):
    key = jax.random.fold_in(key, 7)
    first_key, second_key, third_key = jax.random.split(key, 3)
    owner_rows = N_DP * N_TABLE
    load_level = jax.random.randint(first_key, (owner_rows, 1), 1, 5)
    base_count = jax.random.randint(second_key, (owner_rows, N_TABLE), max(CAP // 4, 1), CAP + 1)
    counts = jnp.maximum(base_count * load_level // 4, 1)
    chosen = jax.random.randint(third_key, (), 0, owner_rows * N_TABLE)
    filled = counts.reshape(-1).at[chosen].set(CAP)
    return filled.reshape(owner_rows, N_TABLE).astype(jnp.int32)


def place_ends(drawn, stream_key, smallest, high):
    place = [jax.random.randint(jax.random.fold_in(stream_key, axis), (), 0, length) for axis, length in enumerate(drawn.shape)]
    widest = drawn.shape.index(max(drawn.shape))
    beside = place[:widest] + [(place[widest] + 1) % drawn.shape[widest]] + place[widest + 1:]
    return drawn.at[tuple(place)].set(smallest).at[tuple(beside)].set(high)


def level_of(stream_key, shape, shards, smallest, high):
    def one(axis_at, blocks):
        steps = jax.random.uniform(jax.random.fold_in(jax.random.fold_in(stream_key, 6), axis_at), (blocks,), jnp.float32, smallest / len(shards), high / len(shards))
        return jnp.repeat(jnp.exp(steps), shape[axis_at] // blocks).reshape((-1,) + (1,) * (len(shape) - axis_at - 1))

    factor_of = one(*shards[0])
    for cut in shards[1:]:
        factor_of = factor_of * one(*cut)
    return factor_of


def cumulative_ranks(amount, slope):
    loads = [(1 << 20) // math.isqrt(grade ** slope) + 1 for grade in range(1, amount + 1)]
    deviation = 1 + sum(loads) // (1 << 30)
    return np.cumsum(np.array([max(1, weight // deviation) for weight in loads]))


def ranked_ids(key, extent, number_of, slope):
    listing = cumulative_ranks(number_of, slope)
    ticket = jax.random.randint(jax.random.fold_in(key, 1), extent, 0, int(listing[number_of - 1]))
    grade = jnp.searchsorted(jnp.asarray(listing, jnp.int32), ticket, side="right")
    return jax.random.permutation(jax.random.fold_in(key, 2), number_of)[grade].astype(jnp.int32)


def scatter_about(key, shape, deviation, most, shards=(), kind=jnp.bfloat16):
    result = jax.random.normal(key, shape, jnp.float32) * deviation
    if len(shards) > 0:
        result = level_of(key, shape, shards, -0.22, 0.18) * result
    return jnp.clip(result, min=-most, max=most).astype(kind)


def setup_inputs(seed: int = 0) -> dict:
    key_list = jax.random.split(jax.random.key(seed), 17)
    dense_input = scatter_about(key_list[0], (BATCH, DENSE_IN), 1.0, 6.0, ((0, 768),))
    hot_ids = place_ends(ranked_ids(key_list[1], (BATCH, TABLES * LH), HOT, 2), jax.random.fold_in(key_list[1], 3), 0, HOT - 1).astype(jnp.int32)
    logit_grad = scatter_about(key_list[2], (BATCH,), (4.0 / (N_DP * N_TABLE) ** 0.5), 0.875, ((0, 768),), jnp.float32)
    hot_table = scatter_about(key_list[3], (HOT, E), 1.0, 6.0)
    hot_accum = jnp.clip(jnp.exp(jax.random.uniform(key_list[4], (HOT,), jnp.float32, math.log(0.03), math.log(1.0))), 0.03, 1.0)
    cold_table = scatter_about(key_list[5], (COLD, E), 1.0, 6.0, ((0, 768),))
    cold_accum = jnp.clip(jnp.exp(math.log(0.00013020834) - 3.506558 * jax.random.uniform(key_list[6], (COLD,), jnp.float32) ** level_of(key_list[6], (COLD,), ((0, 768),), -0.2, 0.2)), 3.906250185536919e-06, 0.00013020834)
    send_rows = place_ends(jax.random.randint(key_list[7], (N_DP * N_TABLE * N_TABLE, CAP), 0, ROWS_DEV), jax.random.fold_in(key_list[7], 1), 0, ROWS_DEV - 1).astype(jnp.int32)
    send_count = draw_send_count(jax.random.fold_in(key_list[16], 71), 0)
    recv_bags = place_ends(jax.random.randint(key_list[9], (N_DP * N_TABLE * N_TABLE, CAP), 0, B_DEV * TABLES), jax.random.fold_in(key_list[9], 1), 0, (B_DEV * TABLES) - 1).astype(jnp.int32)
    bottom_one = scatter_about(key_list[10], (DENSE_IN, BOT1), DENSE_IN ** -0.5, 1.75)
    bottom_two = scatter_about(key_list[11], (BOT1, BOT2), BOT1 ** -0.5, 0.25)
    bottom_three = scatter_about(key_list[12], (BOT2, E), BOT2 ** -0.5, 0.375)
    cross_down = scatter_about(key_list[13], (F, R), F ** -0.5, 0.109375)
    cross_up = scatter_about(key_list[14], (R, F), R ** -0.5, 0.25)
    head_vector = scatter_about(key_list[15], (F,), F ** -0.5, 0.109375, (), jnp.float32)
    return dict(dense_input=dense_input, hot_ids=hot_ids, logit_grad=logit_grad, hot_table=hot_table, hot_accum=hot_accum, cold_table=cold_table, cold_accum=cold_accum, send_rows=send_rows, send_count=send_count, recv_bags=recv_bags, bottom_one=bottom_one, bottom_two=bottom_two, bottom_three=bottom_three, cross_down=cross_down, cross_up=cross_up, head_vector=head_vector)


def forward_backward(features, hot_index, cold_pool, hot_table, bottom_one, bottom_two, bottom_three, cross_down, cross_up, head_vector, upstream_grad):
    samples = features.shape[0]
    first_act = jax.nn.relu(jnp.dot(features, bottom_one, preferred_element_type=jnp.float32)).astype(jnp.bfloat16)
    second_act = jax.nn.relu(jnp.dot(first_act, bottom_two, preferred_element_type=jnp.float32)).astype(jnp.bfloat16)
    bottom_out = jax.nn.relu(jnp.dot(second_act, bottom_three, preferred_element_type=jnp.float32))
    looked_up = hot_table[hot_index].astype(jnp.float32).reshape(samples, TABLES, LH, E).sum(axis=2)
    pooled = looked_up + cold_pool.reshape(samples, TABLES, E)
    inputs_cross = jnp.concatenate([bottom_out, pooled.reshape(samples, TABLES * E)], axis=1).astype(jnp.bfloat16)
    lowrank = jnp.dot(inputs_cross, cross_down, preferred_element_type=jnp.float32).astype(jnp.bfloat16)
    crossed = jnp.dot(lowrank, cross_up, preferred_element_type=jnp.float32)
    widened = inputs_cross.astype(jnp.float32)
    gated = crossed + 1.0
    logits = lax.optimization_barrier(jnp.sum(widened * gated * head_vector[None, :], axis=1))
    outer_grad = upstream_grad[:, None] * head_vector[None, :]
    cross_grad = (outer_grad * widened).astype(jnp.bfloat16)
    lowrank_grad = lax.dot_general(cross_grad, cross_up, (((1,), (1,)), ((), ())), preferred_element_type=jnp.float32).astype(jnp.bfloat16)
    input_grad = outer_grad * gated + lax.dot_general(lowrank_grad, cross_down, (((1,), (1,)), ((), ())), preferred_element_type=jnp.float32)
    bag_grad = input_grad[:, E:].astype(jnp.bfloat16).reshape(samples, TABLES, E)
    return (logits, bag_grad)

def hot_partial(bag_grad, hot_index):
    samples = bag_grad.shape[0]
    spread = jnp.broadcast_to(bag_grad[:, :, None, :].astype(jnp.float32), (samples, TABLES, LH, E)).reshape(-1, E)
    return jax.ops.segment_sum(spread, hot_index.reshape(-1).astype(jnp.int32), num_segments=HOT)

def adagrad_rows(table_rows, accum_rows, gradient):
    updated_accum = accum_rows + lax.optimization_barrier(jnp.mean(gradient * gradient, axis=1))
    return table_rows.astype(jnp.float32) - 1.0 * gradient / jnp.sqrt(updated_accum)[:, None]

def reference(dense_input, hot_ids, logit_grad, hot_table, hot_accum, cold_table, cold_accum, send_rows, send_count, recv_bags, bottom_one, bottom_two, bottom_three, cross_down, cross_up, head_vector):
    group_rows = N_TABLE * ROWS_DEV
    group_bags = N_TABLE * B_DEV * TABLES
    owners = jnp.arange(N_TABLE, dtype=jnp.int32)
    slot_index = jnp.arange(CAP, dtype=jnp.int32)

    def one_group(hot_total, pieces):
        features, hot_index, upstream, cold_block, sends, counts, bags = pieces
        row_index = (owners[:, None, None] * ROWS_DEV + sends).astype(jnp.int32)
        alive = slot_index[None, None, :] < counts[:, :, None]
        picked = cold_block[row_index]
        outgoing = jnp.where(alive[..., None], picked, jnp.zeros_like(picked))
        bag_index = (owners[:, None, None] * (B_DEV * TABLES) + bags).astype(jnp.int32)
        arrived = jnp.transpose(outgoing, (1, 0, 2, 3))
        cold_pool = jax.ops.segment_sum(arrived.reshape(-1, E).astype(jnp.float32), bag_index.reshape(-1), num_segments=group_bags)
        logits, bag_grad = forward_backward(features, hot_index, cold_pool, hot_table, bottom_one, bottom_two, bottom_three, cross_down, cross_up, head_vector, upstream)
        slot_grad = bag_grad.reshape(-1, E)[bag_index]
        returned = jnp.transpose(slot_grad, (1, 0, 2, 3)).astype(jnp.float32)
        masked = jnp.where(alive[..., None], returned, jnp.zeros_like(returned))
        cold_grad = jax.ops.segment_sum(masked.reshape(-1, E), row_index.reshape(-1), num_segments=group_rows)
        return (hot_total + hot_partial(bag_grad, hot_index), (logits, cold_grad))
    pieces = (dense_input.reshape(N_DP, N_TABLE * B_DEV, DENSE_IN), hot_ids.reshape(N_DP, N_TABLE * B_DEV, TABLES * LH), logit_grad.reshape(N_DP, N_TABLE * B_DEV), cold_table.reshape(N_DP, group_rows, E), send_rows.reshape(N_DP, N_TABLE, N_TABLE, CAP), send_count.reshape(N_DP, N_TABLE, N_TABLE), recv_bags.reshape(N_DP, N_TABLE, N_TABLE, CAP))
    hot_grad, outputs = lax.scan(one_group, jnp.zeros((HOT, E), jnp.float32), pieces)
    logits, cold_grad = outputs
    new_hot = adagrad_rows(hot_table, hot_accum, hot_grad)
    new_cold = adagrad_rows(cold_table, cold_accum, cold_grad.reshape(-1, E))
    return (logits.reshape(-1), new_hot, new_cold)
```

```python
import jax
import jax.numpy as jnp
from jax import lax
from jax.experimental import pallas as pl
from jax.experimental.pallas import tpu as pltpu
from jax.sharding import PartitionSpec as P

E = 128
TABLES = 26
HALF = 13
LH = 2
HOT = 3072
B = 128
ROWS = 512
CAP = 256
NT = 12
SLOTS = NT * CAP
BAGS = B * TABLES
HB = B * HALF
R = 512
F = 3456
f32 = jnp.float32
bf = jnp.bfloat16
VLIM = 56 * 1024 * 1024
VM = pl.BlockSpec(memory_space=pltpu.VMEM)
SM = pl.BlockSpec(memory_space=pltpu.SMEM)
ANY = pl.BlockSpec(memory_space=pl.ANY)


def dot(a, b):
    return jnp.dot(a, b, preferred_element_type=f32)


def dot_t(a, b):
    return lax.dot_general(a, b, (((1,), (1,)), ((), ())), preferred_element_type=f32)


def hit(idx, base, shape, axis):
    place = lax.broadcasted_iota(jnp.int32, shape, axis)
    return jnp.where(idx - base == place, 1.0, 0.0).astype(bf)


def call(kernel, outs, n_in_specs, scratch=(), flops=0, nbytes=0):
    return pl.pallas_call(
        kernel,
        out_shape=outs,
        in_specs=n_in_specs,
        out_specs=jax.tree.map(lambda _: VM, outs),
        scratch_shapes=list(scratch),
        compiler_params=pltpu.CompilerParams(vmem_limit_bytes=VLIM),
        cost_estimate=pl.CostEstimate(flops=flops, bytes_accessed=nbytes, transcendentals=0),
    )


def split_bag(bag):
    sample = (bag * 2521) >> 16
    table = bag - sample * TABLES
    upper = table >= HALF
    return upper, jnp.where(upper, table - HALF, table) * B + sample


def pick_kernel(count_ref, rows_ref, table_ref, out_ref, wide):
    wide[:, :E] = table_ref[: ROWS // 2, :]
    wide[:, E:] = table_ref[ROWS // 2 :, :]
    slot = lax.broadcasted_iota(jnp.int32, (CAP, 1), 0)
    for s in range(NT):
        row = rows_ref[:, s : s + 1]
        row = jnp.where(slot < count_ref[0, s], row, -1)
        upper = row >= ROWS // 2
        low = jnp.where(upper, row - ROWS // 2, row)
        both = dot(hit(low, 0, (CAP, ROWS // 2), 1), wide[...])
        out_ref[s * CAP : (s + 1) * CAP, :] = jnp.where(upper, both[:, E:], both[:, :E]).astype(bf)


def hot_kernel(ids_ref, table_ref, dense_ref, one_ref, two_ref, three_ref, out_ref, bottom_ref):
    first = jnp.maximum(dot(dense_ref[...], one_ref[...]), 0.0).astype(bf)
    second = jnp.maximum(dot(first, two_ref[...]), 0.0).astype(bf)
    bottom_ref[...] = jnp.maximum(dot(second, three_ref[...]), 0.0).astype(bf)

    def pair(j, _):
        ids = pltpu.roll(ids_ref[...], lax.rem(128 - 4 * j, 128), 1)
        left = jnp.concatenate([ids[:, 0:1], ids[:, 2:3]], axis=0)
        right = jnp.concatenate([ids[:, 1:2], ids[:, 3:4]], axis=0)
        count = hit(left, 0, (2 * B, HOT), 1) + hit(right, 0, (2 * B, HOT), 1)
        out_ref[pl.ds(pl.multiple_of(j * 2 * B, 2 * B), 2 * B), :] = dot(count, table_ref[...])
        return 0

    lax.fori_loop(0, HALF, pair, 0)


M_POOL = 416


def cross_kernel(
    hot_ref,
    bottom_ref,
    arrived_ref,
    bags_ref,
    bags_t_ref,
    grad_ref,
    head_ref,
    down_hbm,
    up_hbm,
    logits_ref,
    bag_grad_ref,
    slot_ref,
    down,
    up,
    wide,
    cold,
    x0,
    sems,
):
    copy_down = pltpu.make_async_copy(down_hbm, down, sems.at[0])
    copy_up = pltpu.make_async_copy(up_hbm, up, sems.at[1])
    copy_down.start()
    copy_up.start()
    zero = jnp.zeros((CAP, E), bf)
    for s in range(NT):
        upper, _ = split_bag(bags_t_ref[:, s : s + 1])
        block = arrived_ref[s * CAP : (s + 1) * CAP, :]
        wide[s * CAP : (s + 1) * CAP, :E] = jnp.where(upper, zero, block)
        wide[s * CAP : (s + 1) * CAP, E:] = jnp.where(upper, block, zero)
    _, place = split_bag(bags_ref[...])

    def pool(j, _):
        base = j * M_POOL
        flat = jnp.concatenate([place[s : s + 1, :] for s in range(NT)], axis=1)
        part = dot(hit(flat, base, (M_POOL, SLOTS), 0), wide[...])
        cold[pl.ds(pl.multiple_of(base, M_POOL), M_POOL), :] = part
        return 0

    lax.fori_loop(0, HB // M_POOL, pool, 0)
    x0[:, :E] = bottom_ref[...]
    for t in range(TABLES):
        r = (t % HALF) * B
        c = (t // HALF) * E
        x0[:, E * (t + 1) : E * (t + 2)] = (
            hot_ref[t * B : (t + 1) * B, :] + cold[r : r + B, c : c + E]
        ).astype(bf)
    copy_down.wait()
    copy_up.wait()
    low = dot(x0[...], down[...]).astype(bf)
    upstream = grad_ref[...]
    total = jnp.zeros((B, E), f32)
    low_grad = jnp.zeros((B, R), f32)
    for k in range(TABLES + 1):
        cols = slice(E * k, E * (k + 1))
        head = head_ref[:, cols]
        wide_x = x0[:, cols].astype(f32)
        gated = dot(low, up[:, cols]) + 1.0
        total = total + wide_x * gated * head
        outer = upstream * head
        low_grad = low_grad + dot_t((outer * wide_x).astype(bf), up[:, cols])
        if k > 0:
            t = k - 1
            r = (t % HALF) * B
            c = (t // HALF) * E
            cold[r : r + B, c : c + E] = outer * gated
    logits_ref[...] = jnp.sum(total, axis=1, keepdims=True)
    low_grad = low_grad.astype(bf)
    for t in range(TABLES):
        r = (t % HALF) * B
        c = (t // HALF) * E
        part = dot_t(low_grad, down[E * (t + 1) : E * (t + 2), :])
        bag_grad_ref[r : r + B, c : c + E] = (cold[r : r + B, c : c + E] + part).astype(bf)


def slot_kernel(bags_t_ref, bag_grad_ref, slot_ref):
    for s in range(NT):
        upper, place_s = split_bag(bags_t_ref[:, s : s + 1])
        both = dot(hit(place_s, 0, (CAP, HB), 1), bag_grad_ref[...])
        slot_ref[s * CAP : (s + 1) * CAP, :] = jnp.where(upper, both[:, E:], both[:, :E]).astype(bf)


M_HOT = 256


def hot_grad_kernel(ids_t_ref, bag_grad_ref, out_ref, stack):
    for t in range(TABLES):
        r = (t % HALF) * B
        c = (t // HALF) * E
        stack[t * B : (t + 1) * B, :] = bag_grad_ref[r : r + B, c : c + E]
    left = jnp.concatenate([ids_t_ref[2 * t : 2 * t + 1, :] for t in range(TABLES)], axis=1)
    right = jnp.concatenate([ids_t_ref[2 * t + 1 : 2 * t + 2, :] for t in range(TABLES)], axis=1)

    def rows(j, _):
        base = j * M_HOT
        count = hit(left, base, (M_HOT, BAGS), 0) + hit(right, base, (M_HOT, BAGS), 0)
        out_ref[pl.ds(pl.multiple_of(base, M_HOT), M_HOT), :] = dot(count, stack[...])
        return 0

    lax.fori_loop(0, HOT // M_HOT, rows, 0)


def cold_kernel(count_ref, rows_ref, returned_ref, table_ref, accum_ref, out_ref):
    lane = lax.broadcasted_iota(jnp.int32, (1, CAP), 1)
    flat = jnp.concatenate(
        [jnp.where(lane < count_ref[0, s], rows_ref[s : s + 1, :], -1) for s in range(NT)], axis=1
    )
    grad = dot(hit(flat, 0, (ROWS, SLOTS), 0), returned_ref[...])
    updated = accum_ref[...] + jnp.mean(grad * grad, axis=1, keepdims=True)
    out_ref[...] = table_ref[...].astype(f32) - grad / jnp.sqrt(updated)


def sds(shape, dtype):
    return jax.ShapeDtypeStruct(shape, dtype)


def pick(count, rows_t, table):
    return call(pick_kernel, sds((SLOTS, E), bf), [SM, VM, VM], [pltpu.VMEM((ROWS // 2, 2 * E), bf)], 2 * SLOTS * ROWS * E, 2000000)(
        count, rows_t, table
    )


def hot_pool(ids, table, dense, one, two, three):
    return call(hot_kernel, (sds((BAGS, E), f32), sds((B, E), bf)), [VM] * 6, (), 2 * BAGS * HOT * E, 4000000)(
        ids, table, dense, one, two, three
    )


def cross(hot, bottom, arrived, bags, bags_t, grad, head, down, up):
    def kernel(*refs):
        cross_kernel(*refs[:11], None, *refs[11:])

    return call(
        kernel,
        (sds((B, 1), f32), sds((HB, 2 * E), bf)),
        [VM] * 7 + [ANY] * 2,
        [
            pltpu.VMEM((F, R), bf),
            pltpu.VMEM((R, F), bf),
            pltpu.VMEM((SLOTS, 2 * E), bf),
            pltpu.VMEM((HB, 2 * E), f32),
            pltpu.VMEM((B, F), bf),
            pltpu.SemaphoreType.DMA((2,)),
        ],
        2 * BAGS * SLOTS * E + 8 * B * F * R,
        12000000,
    )(hot, bottom, arrived, bags, bags_t, grad, head, down, up)


def slot_grads(bags_t, bag_grad):
    return call(slot_kernel, sds((SLOTS, E), bf), [VM] * 2, (), 2 * BAGS * SLOTS * E, 2000000)(bags_t, bag_grad)


def hot_sum(ids_t, bag_grad):
    return call(hot_grad_kernel, sds((HOT, E), f32), [VM] * 2, [pltpu.VMEM((BAGS, E), bf)], 2 * BAGS * HOT * E, 3000000)(ids_t, bag_grad)


def cold_update(count, rows, returned, table, accum):
    return call(cold_kernel, sds((ROWS, E), f32), [SM] + [VM] * 4, (), 2 * ROWS * SLOTS * E, 2000000)(
        count, rows, returned, table, accum
    )


def a2a(v, axis, groups=None):
    return lax.all_to_all(v, axis, split_axis=0, concat_axis=0, tiled=True, axis_index_groups=groups)


def body(
    dense_input,
    hot_ids,
    logit_grad,
    hot_table,
    hot_accum,
    cold_table,
    cold_accum,
    send_rows,
    send_count,
    recv_bags,
    bottom_one,
    bottom_two,
    bottom_three,
    cross_down,
    cross_up,
    head_vector,
):
    n_dp = lax.axis_size("dp")
    n_xy = n_dp // 2
    xy_groups = [[2 * k + c for k in range(n_xy)] for c in range(2)]
    twin = [(i, i ^ 1) for i in range(n_dp)]
    outgoing = pick(send_count, send_rows.T, cold_table)
    arrived = a2a(outgoing, "table")
    bags_t = recv_bags.T
    ids = jnp.pad(hot_ids, ((0, 0), (0, 128 - TABLES * LH)))
    hot, bottom = hot_pool(ids, hot_table, dense_input, bottom_one, bottom_two, bottom_three)
    logits, bag_grad = cross(
        hot, bottom, arrived, recv_bags, bags_t, logit_grad[:, None], head_vector[None, :], cross_down, cross_up
    )
    hot_local = hot_sum(hot_ids.T, bag_grad)
    core = lax.rem(lax.axis_index("dp"), 2)
    half = HOT // 2
    mine = lax.dynamic_slice_in_dim(hot_local, core * half, half, 0)
    other = lax.dynamic_slice_in_dim(hot_local, (1 - core) * half, half, 0).astype(bf)
    met = lax.ppermute(other, "dp", twin)
    slot_grad = slot_grads(bags_t, bag_grad)
    returned = a2a(slot_grad, "table")
    chip = (mine + met.astype(f32)).astype(bf)
    share = half // n_xy
    plane = a2a(chip, "dp", xy_groups)
    plane = jnp.sum(plane.reshape(n_xy, share, E).astype(f32), axis=0).astype(bf)
    column = a2a(jnp.broadcast_to(plane[None], (NT, share, E)).reshape(NT * share, E), "table")
    grad = jnp.sum(column.reshape(NT, share, E).astype(f32), axis=0)
    first = core * half + lax.div(lax.axis_index("dp"), 2) * share
    accum = lax.dynamic_slice_in_dim(hot_accum, first, share, 0)
    step = grad / jnp.sqrt(accum + jnp.mean(grad * grad, axis=1))[:, None]
    step = step.astype(bf)
    steps = a2a(jnp.broadcast_to(step[None], (n_xy, share, E)).reshape(half, E), "dp", xy_groups)
    others = lax.ppermute(steps, "dp", twin)
    low = jnp.where(core == 0, steps, others)
    high = jnp.where(core == 0, others, steps)
    new_hot = hot_table.astype(f32) - jnp.concatenate([low, high], axis=0).astype(f32)
    new_cold = cold_update(send_count, send_rows, returned, cold_table, cold_accum[:, None])
    return (logits[:, 0], new_hot, new_cold)


def solution(mesh):
    rows = P(("dp", "table"), None)
    flat = P(("dp", "table"))
    return jax.shard_map(
        body,
        mesh=mesh,
        in_specs=(rows, rows, flat, P(), P(), rows, flat, rows, rows, rows, P(), P(), P(), P(), P(), P()),
        out_specs=(flat, P(), rows),
        check_vma=False,
    )
```

```python
import jax
import jax.numpy as jnp
from jax import lax
from jax.experimental import pallas as pl
from jax.experimental.pallas import tpu as pltpu
from jax.sharding import PartitionSpec as P

E = 128
TABLES = 26
HALF = 13
LH = 2
HOT = 3072
B = 128
ROWS = 512
CAP = 256
NT = 12
SLOTS = NT * CAP
BAGS = B * TABLES
HB = B * HALF
R = 512
F = 3456
f32 = jnp.float32
bf = jnp.bfloat16
MIB = 1024 * 1024
VM = pl.BlockSpec(memory_space=pltpu.VMEM)
ANY = pl.BlockSpec(memory_space=pl.ANY)
SM = pl.BlockSpec(memory_space=pltpu.SMEM)


def dot(a, b):
    return jnp.dot(a, b, preferred_element_type=f32)


def dot_t(a, b):
    return lax.dot_general(a, b, (((1,), (1,)), ((), ())), preferred_element_type=f32)


def hit(idx, base, shape, axis):
    place = lax.broadcasted_iota(jnp.int32, shape, axis)
    return jnp.where(idx - base == place, 1.0, 0.0).astype(bf)


def call(kernel, outs, n_in_specs, scratch=(), flops=0, nbytes=0, mib=24):
    return pl.pallas_call(
        kernel,
        out_shape=outs,
        in_specs=n_in_specs,
        out_specs=jax.tree.map(lambda _: VM, outs),
        scratch_shapes=list(scratch),
        compiler_params=pltpu.CompilerParams(vmem_limit_bytes=mib * MIB),
        cost_estimate=pl.CostEstimate(flops=flops, bytes_accessed=nbytes, transcendentals=0),
    )


def split_bag(bag):
    sample = (bag * 2521) >> 16
    table = bag - sample * TABLES
    upper = table >= HALF
    return upper, jnp.where(upper, table - HALF, table) * B + sample


def pick_kernel(count_ref, rows_ref, table_ref, out_ref, wide):
    rows_t = rows_ref[...].T
    wide[:, :E] = table_ref[: ROWS // 2, :]
    wide[:, E:] = table_ref[ROWS // 2 :, :]
    slot = lax.broadcasted_iota(jnp.int32, (CAP, 1), 0)
    for s in range(NT):
        row = rows_t[:, s : s + 1]
        row = jnp.where(slot < count_ref[0, s], row, -1)
        upper = row >= ROWS // 2
        low = jnp.where(upper, row - ROWS // 2, row)
        both = dot(hit(low, 0, (CAP, ROWS // 2), 1), wide[...])
        out_ref[s * CAP : (s + 1) * CAP, :] = jnp.where(upper, both[:, E:], both[:, :E]).astype(bf)


def hot_kernel(ids_ref, table_ref, dense_ref, one_ref, two_ref, three_ref, out_ref, bottom_ref):
    first = jnp.maximum(dot(dense_ref[...], one_ref[...]), 0.0).astype(bf)
    second = jnp.maximum(dot(first, two_ref[...]), 0.0).astype(bf)
    bottom_ref[...] = jnp.maximum(dot(second, three_ref[...]), 0.0).astype(bf)

    def pair(j, _):
        ids = pltpu.roll(ids_ref[...], lax.rem(128 - 4 * j, 128), 1)
        left = jnp.concatenate([ids[:, 0:1], ids[:, 2:3]], axis=0)
        right = jnp.concatenate([ids[:, 1:2], ids[:, 3:4]], axis=0)
        count = hit(left, 0, (2 * B, HOT), 1) + hit(right, 0, (2 * B, HOT), 1)
        out_ref[pl.ds(pl.multiple_of(j * 2 * B, 2 * B), 2 * B), :] = dot(count, table_ref[...])
        return 0

    lax.fori_loop(0, HALF, pair, 0)


HK = 4
HQ = HOT // HK
HT = 26
SG = 4


def mark(idx, shape, axis):
    place = lax.broadcasted_iota(jnp.int16, shape, axis)
    return jnp.where(idx.astype(jnp.int16) == place, jnp.ones(shape, bf), jnp.zeros(shape, bf))


def spot(t):
    r = (t % HALF) * B
    c = (t // HALF) * E
    return slice(r, r + B), slice(c, c + E)


def cross_kernel(
    hot_ref,
    bottom_ref,
    arrived_ref,
    bags_ref,
    bags_t_ref,
    grad_ref,
    head_ref,
    down_hbm,
    up_hbm,
    logits_ref,
    bag_grad_ref,
    slot_ref,
    down,
    up,
    cold,
    x0,
    sems,
):
    copy_down = pltpu.make_async_copy(down_hbm, down, sems.at[0])
    copy_up = pltpu.make_async_copy(up_hbm, up, sems.at[1])
    copy_down.start()
    copy_up.start()
    zero = jnp.zeros((CAP, E), bf)
    _, place = split_bag(bags_ref[...])
    for g in range(2):
        owners = range(6 * g, 6 * g + 6)
        wide = []
        for s in owners:
            upper, _ = split_bag(bags_t_ref[:, s : s + 1])
            block = arrived_ref[s * CAP : (s + 1) * CAP, :]
            wide.append(jnp.concatenate([jnp.where(upper, zero, block), jnp.where(upper, block, zero)], axis=1))
        flat = jnp.concatenate([place[s : s + 1, :] for s in owners], axis=1)
        part = dot(mark(flat, (HB, 6 * CAP), 0), jnp.concatenate(wide, axis=0))
        cold[...] = part if g == 0 else cold[...] + part
    x0[:, :E] = bottom_ref[...]
    for t in range(TABLES):
        r, c = spot(t)
        x0[:, E * (t + 1) : E * (t + 2)] = (hot_ref[t * B : (t + 1) * B, :] + cold[r, c]).astype(bf)
    upstream = grad_ref[...]
    copy_down.wait()
    copy_up.wait()
    low = dot(x0[...], down[...]).astype(bf)
    low_grad = dot_t((upstream * head_ref[...] * x0[...].astype(f32)).astype(bf), up[...]).astype(bf)
    logit = jnp.zeros((B, E), f32)
    for k in range(0, TABLES + 1, 3):
        cols = slice(E * k, E * (k + 3))
        head = head_ref[:, cols]
        gated = dot(low, up[:, cols]) + 1.0
        part = x0[:, cols].astype(f32) * gated * head
        logit = logit + part[:, :E] + part[:, E : 2 * E] + part[:, 2 * E :]
        back = upstream * head * gated + dot_t(low_grad, down[cols, :])
        for i in range(3):
            if k + i > 0:
                r, c = spot(k + i - 1)
                bag_grad_ref[r, c] = back[:, E * i : E * (i + 1)].astype(bf)
    logits_ref[...] = jnp.sum(logit, axis=1, keepdims=True)
    for g in range(0, NT, SG):
        halves, marks = [], []
        for s in range(g, g + SG):
            upper, place = split_bag(bags_t_ref[:, s : s + 1])
            halves.append(upper)
            marks.append(hit(place, 0, (CAP, HB), 1))
        both = dot(jnp.concatenate(marks, axis=0), bag_grad_ref[...])
        upper = jnp.concatenate(halves, axis=0)
        slot_ref[g * CAP : (g + SG) * CAP, :] = jnp.where(upper, both[:, E:], both[:, :E]).astype(bf)


def hot_grad_kernel(core_ref, bag_grad_ref, ids_ref, ids_t_ref, mine_ref, other_ref, total):
    none = jnp.zeros((B, E), bf)
    low_ids = lax.rem(ids_t_ref[...], HQ)
    for g in range(TABLES * LH // HT):
        places, blocks = [], []
        for i in range(HT):
            n = g * HT + i
            r, c = spot(n // LH)
            block = bag_grad_ref[r, c]
            col = ids_ref[:, n : n + 1]
            blocks.append(
                jnp.concatenate(
                    [jnp.where((col >= q * HQ) & (col < (q + 1) * HQ), block, none) for q in range(HK)], axis=1
                )
            )
            places.append(low_ids[n : n + 1, :])
        part = dot(
            mark(jnp.concatenate(places, axis=1), (HQ, HT * B), 0), jnp.concatenate(blocks, axis=0)
        )
        total[...] = part if g == 0 else total[...] + part
    first = core_ref[0] == 0
    for q in range(HK // 2):
        lower = total[:, q * E : (q + 1) * E]
        higher = total[:, (q + HK // 2) * E : (q + HK // 2 + 1) * E]
        rows = slice(q * HQ, (q + 1) * HQ)
        mine_ref[rows, :] = jnp.where(first, lower, higher)
        other_ref[rows, :] = jnp.where(first, higher, lower).astype(bf)


def share_kernel(x_ref, mine_ref, met_ref, own_ref, one_ref, two_ref, three_ref):
    part = own_ref.shape[0]
    for k, out in enumerate((own_ref, one_ref, two_ref, three_ref)):
        start = pl.multiple_of(lax.rem(x_ref[0] + k, 4) * part, part)
        chip = mine_ref[pl.ds(start, part), :] + met_ref[pl.ds(start, part), :].astype(f32)
        out[...] = chip.astype(out.dtype)


def cold_kernel(count_ref, rows_ref, returned_ref, table_ref, accum_ref, out_ref):
    lane = lax.broadcasted_iota(jnp.int32, (1, CAP), 1)
    flat = jnp.concatenate(
        [jnp.where(lane < count_ref[0, s], rows_ref[s : s + 1, :], -1) for s in range(NT)], axis=1
    )
    grad = dot(hit(flat, 0, (ROWS, SLOTS), 0), returned_ref[...])
    updated = accum_ref[...] + jnp.mean(grad * grad, axis=1, keepdims=True)
    out_ref[...] = table_ref[...].astype(f32) - grad / jnp.sqrt(updated)


def sds(shape, dtype):
    return jax.ShapeDtypeStruct(shape, dtype)


def pick(count, rows_t, table):
    return call(pick_kernel, sds((SLOTS, E), bf), [SM, VM, VM], [pltpu.VMEM((ROWS // 2, 2 * E), bf)], 2 * SLOTS * ROWS * E, 2000000)(
        count, rows_t, table
    )


def hot_pool(ids, table, dense, one, two, three):
    return call(hot_kernel, (sds((BAGS, E), f32), sds((B, E), bf)), [VM] * 6, (), 2 * BAGS * HOT * E, 4000000)(
        ids, table, dense, one, two, three
    )


def cross(hot, bottom, arrived, bags, bags_t, grad, head, down, up):
    return call(
        cross_kernel,
        (sds((B, 1), f32), sds((HB, 2 * E), bf), sds((SLOTS, E), bf)),
        [VM] * 7 + [ANY] * 2,
        [
            pltpu.VMEM((F, R), bf),
            pltpu.VMEM((R, F), bf),
            pltpu.VMEM((HB, 2 * E), f32),
            pltpu.VMEM((B, F), bf),
            pltpu.SemaphoreType.DMA((2,)),
        ],
        4 * BAGS * SLOTS * E + 8 * B * F * R,
        14000000,
        60,
    )(hot, bottom, arrived, bags, bags_t, grad, head, down, up)


def hot_sum(core, bag_grad, ids, ids_t):
    return call(
        hot_grad_kernel,
        (sds((HOT // 2, E), f32), sds((HOT // 2, E), bf)),
        [SM] + [VM] * 3,
        [pltpu.VMEM((HQ, HK * E), f32)],
        2 * BAGS * HOT * E,
        3000000,
        32,
    )(core, bag_grad, ids, ids_t)


def shares(x, mine, met):
    part = HOT // 8
    return call(
        share_kernel,
        (sds((part, E), f32),) + (sds((part, E), bf),) * 3,
        [SM] + [VM] * 2,
        (),
        HOT * E,
        2000000,
    )(x, mine, met)


def cold_update(count, rows, returned, table, accum):
    return call(cold_kernel, sds((ROWS, E), f32), [SM] + [VM] * 4, (), 2 * ROWS * SLOTS * E, 2000000)(
        count, rows, returned, table, accum
    )


def a2a(v, axis, groups=None):
    return lax.all_to_all(v, axis, split_axis=0, concat_axis=0, tiled=True, axis_index_groups=groups)


def body(
    dense_input,
    hot_ids,
    logit_grad,
    hot_table,
    hot_accum,
    cold_table,
    cold_accum,
    send_rows,
    send_count,
    recv_bags,
    bottom_one,
    bottom_two,
    bottom_three,
    cross_down,
    cross_up,
    head_vector,
):
    n_dp = lax.axis_size("dp")
    n_xy = n_dp // 2
    n_y = n_xy // 4
    xy_groups = [[2 * k + c for k in range(n_xy)] for c in range(2)]
    y_groups = [[2 * n_y * x + 2 * y + c for y in range(n_y)] for x in range(4) for c in range(2)]
    twin = [(i, i ^ 1) for i in range(n_dp)]
    outgoing = pick(send_count, send_rows, cold_table)
    arrived = a2a(outgoing, "table")
    bags_t = recv_bags.T
    ids = jnp.pad(hot_ids, ((0, 0), (0, 128 - TABLES * LH)))
    hot, bottom = hot_pool(ids, hot_table, dense_input, bottom_one, bottom_two, bottom_three)
    core = lax.rem(lax.axis_index("dp"), 2)
    x_at = lax.div(lax.axis_index("dp"), 2 * n_y)
    half = HOT // 2
    logits, bag_grad, slot_grad = cross(
        hot, bottom, arrived, recv_bags, bags_t, logit_grad[:, None], head_vector[None, :], cross_down, cross_up
    )
    returned = a2a(slot_grad, "table")
    mine, other = hot_sum(core[None], bag_grad, hot_ids, hot_ids.T)
    met = lax.ppermute(other, "dp", twin)
    total, *parts = shares(x_at[None], mine, met)
    for k in range(1, 4):
        ahead = [(i, (i + 2 * n_y * k) % n_dp) for i in range(n_dp)]
        total = total + lax.ppermute(parts[k - 1], "dp", ahead).astype(f32)
    total, returned = lax.optimization_barrier((total.astype(bf), returned))
    share = half // n_xy
    line = a2a(total, "dp", y_groups)
    plane = jnp.sum(line.reshape(n_y, share, E).astype(f32), axis=0).astype(bf)
    column = a2a(jnp.broadcast_to(plane[None], (NT, share, E)).reshape(NT * share, E), "table")
    grad = jnp.sum(column.reshape(NT, share, E).astype(f32), axis=0)
    first = core * half + lax.div(lax.axis_index("dp"), 2) * share
    accum = lax.dynamic_slice_in_dim(hot_accum, first, share, 0)
    step = grad / jnp.sqrt(accum + jnp.mean(grad * grad, axis=1))[:, None]
    step = step.astype(bf)
    steps = a2a(jnp.broadcast_to(step[None], (n_xy, share, E)).reshape(half, E), "dp", xy_groups)
    others = lax.ppermute(steps, "dp", twin)
    low = jnp.where(core == 0, steps, others)
    high = jnp.where(core == 0, others, steps)
    new_hot = hot_table.astype(f32) - jnp.concatenate([low, high], axis=0).astype(f32)
    new_cold = cold_update(send_count, send_rows, returned, cold_table, cold_accum[:, None])
    return (logits[:, 0], new_hot, new_cold)


def solution(mesh):
    rows = P(("dp", "table"), None)
    flat = P(("dp", "table"))
    return jax.shard_map(
        body,
        mesh=mesh,
        in_specs=(rows, rows, flat, P(), P(), rows, flat, rows, rows, rows, P(), P(), P(), P(), P(), P()),
        out_specs=(flat, P(), rows),
        check_vma=False,
    )
```

```python
import jax
import jax.numpy as jnp
from jax import lax
from jax.experimental import pallas as pl
from jax.experimental.pallas import tpu as pltpu
from jax.sharding import PartitionSpec as P

E = 128
TABLES = 26
HALF = 13
LH = 2
HOT = 3072
B = 128
ROWS = 512
CAP = 256
NT = 12
SLOTS = NT * CAP
BAGS = B * TABLES
HB = B * HALF
R = 512
F = 3456
f32 = jnp.float32
bf = jnp.bfloat16
MIB = 1024 * 1024
VM = pl.BlockSpec(memory_space=pltpu.VMEM)
ANY = pl.BlockSpec(memory_space=pl.ANY)
SM = pl.BlockSpec(memory_space=pltpu.SMEM)


def dot(a, b):
    return jnp.dot(a, b, preferred_element_type=f32)


def dot_t(a, b):
    return lax.dot_general(a, b, (((1,), (1,)), ((), ())), preferred_element_type=f32)


def hit(idx, base, shape, axis):
    place = lax.broadcasted_iota(jnp.int32, shape, axis)
    return jnp.where(idx - base == place, 1.0, 0.0).astype(bf)


def call(kernel, outs, n_in_specs, scratch=(), flops=0, nbytes=0, mib=24):
    return pl.pallas_call(
        kernel,
        out_shape=outs,
        in_specs=n_in_specs,
        out_specs=jax.tree.map(lambda _: VM, outs),
        scratch_shapes=list(scratch),
        compiler_params=pltpu.CompilerParams(vmem_limit_bytes=mib * MIB),
        cost_estimate=pl.CostEstimate(flops=flops, bytes_accessed=nbytes, transcendentals=0),
    )


def split_bag(bag):
    sample = (bag * 2521) >> 16
    table = bag - sample * TABLES
    upper = table >= HALF
    return upper, jnp.where(upper, table - HALF, table) * B + sample


def pick_kernel(count_ref, rows_ref, table_ref, out_ref, wide):
    rows_t = rows_ref[...].T
    wide[:, :E] = table_ref[: ROWS // 2, :]
    wide[:, E:] = table_ref[ROWS // 2 :, :]
    slot = lax.broadcasted_iota(jnp.int32, (CAP, 1), 0)
    for s in range(NT):
        row = rows_t[:, s : s + 1]
        row = jnp.where(slot < count_ref[0, s], row, -1)
        upper = row >= ROWS // 2
        low = jnp.where(upper, row - ROWS // 2, row)
        both = dot(hit(low, 0, (CAP, ROWS // 2), 1), wide[...])
        out_ref[s * CAP : (s + 1) * CAP, :] = jnp.where(upper, both[:, E:], both[:, :E]).astype(bf)


def hot_kernel(ids_ref, table_ref, dense_ref, one_ref, two_ref, three_ref, out_ref, bottom_ref):
    first = jnp.maximum(dot(dense_ref[...], one_ref[...]), 0.0).astype(bf)
    second = jnp.maximum(dot(first, two_ref[...]), 0.0).astype(bf)
    bottom_ref[...] = jnp.maximum(dot(second, three_ref[...]), 0.0).astype(bf)

    def pair(j, _):
        ids = pltpu.roll(ids_ref[...], lax.rem(128 - 4 * j, 128), 1)
        left = jnp.concatenate([ids[:, 0:1], ids[:, 2:3]], axis=0)
        right = jnp.concatenate([ids[:, 1:2], ids[:, 3:4]], axis=0)
        count = hit(left, 0, (2 * B, HOT), 1) + hit(right, 0, (2 * B, HOT), 1)
        out_ref[pl.ds(pl.multiple_of(j * 2 * B, 2 * B), 2 * B), :] = dot(count, table_ref[...])
        return 0

    lax.fori_loop(0, HALF, pair, 0)


HK = 4
HQ = HOT // HK
HT = 26
SG = 4


def mark(idx, shape, axis):
    place = lax.broadcasted_iota(jnp.int16, shape, axis)
    return jnp.where(idx.astype(jnp.int16) == place, jnp.ones(shape, bf), jnp.zeros(shape, bf))


def spot(t):
    r = (t % HALF) * B
    c = (t // HALF) * E
    return slice(r, r + B), slice(c, c + E)


def cross_kernel(
    hot_ref,
    bottom_ref,
    arrived_ref,
    bags_ref,
    bags_t_ref,
    grad_ref,
    head_ref,
    down_hbm,
    up_hbm,
    logits_ref,
    bag_grad_ref,
    slot_ref,
    down,
    up,
    cold,
    x0,
    sems,
):
    copy_down = pltpu.make_async_copy(down_hbm, down, sems.at[0])
    copy_up = pltpu.make_async_copy(up_hbm, up, sems.at[1])
    copy_down.start()
    copy_up.start()
    zero = jnp.zeros((CAP, E), bf)
    _, place = split_bag(bags_ref[...])
    for g in range(2):
        owners = range(6 * g, 6 * g + 6)
        wide = []
        for s in owners:
            upper, _ = split_bag(bags_t_ref[:, s : s + 1])
            block = arrived_ref[s * CAP : (s + 1) * CAP, :]
            wide.append(jnp.concatenate([jnp.where(upper, zero, block), jnp.where(upper, block, zero)], axis=1))
        flat = jnp.concatenate([place[s : s + 1, :] for s in owners], axis=1)
        part = dot(mark(flat, (HB, 6 * CAP), 0), jnp.concatenate(wide, axis=0))
        cold[...] = part if g == 0 else cold[...] + part
    x0[:, :E] = bottom_ref[...]
    for t in range(TABLES):
        r, c = spot(t)
        x0[:, E * (t + 1) : E * (t + 2)] = (hot_ref[t * B : (t + 1) * B, :] + cold[r, c]).astype(bf)
    upstream = grad_ref[...]
    copy_down.wait()
    copy_up.wait()
    low = dot(x0[...], down[...]).astype(bf)
    low_grad = dot_t((upstream * head_ref[...] * x0[...].astype(f32)).astype(bf), up[...]).astype(bf)
    logit = jnp.zeros((B, E), f32)
    for k in range(0, TABLES + 1, 3):
        cols = slice(E * k, E * (k + 3))
        head = head_ref[:, cols]
        gated = dot(low, up[:, cols]) + 1.0
        part = x0[:, cols].astype(f32) * gated * head
        logit = logit + part[:, :E] + part[:, E : 2 * E] + part[:, 2 * E :]
        back = upstream * head * gated + dot_t(low_grad, down[cols, :])
        for i in range(3):
            if k + i > 0:
                r, c = spot(k + i - 1)
                bag_grad_ref[r, c] = back[:, E * i : E * (i + 1)].astype(bf)
    logits_ref[...] = jnp.sum(logit, axis=1, keepdims=True)
    for g in range(0, NT, SG):
        halves, marks = [], []
        for s in range(g, g + SG):
            upper, place = split_bag(bags_t_ref[:, s : s + 1])
            halves.append(upper)
            marks.append(hit(place, 0, (CAP, HB), 1))
        both = dot(jnp.concatenate(marks, axis=0), bag_grad_ref[...])
        upper = jnp.concatenate(halves, axis=0)
        slot_ref[g * CAP : (g + SG) * CAP, :] = jnp.where(upper, both[:, E:], both[:, :E]).astype(bf)


def hot_grad_kernel(core_ref, bag_grad_ref, ids_ref, ids_t_ref, mine_ref, other_ref, total):
    none = jnp.zeros((B, E), bf)
    low_ids = lax.rem(ids_t_ref[...], HQ)
    for g in range(TABLES * LH // HT):
        places, blocks = [], []
        for i in range(HT):
            n = g * HT + i
            r, c = spot(n // LH)
            block = bag_grad_ref[r, c]
            col = ids_ref[:, n : n + 1]
            blocks.append(
                jnp.concatenate(
                    [jnp.where((col >= q * HQ) & (col < (q + 1) * HQ), block, none) for q in range(HK)], axis=1
                )
            )
            places.append(low_ids[n : n + 1, :])
        part = dot(
            mark(jnp.concatenate(places, axis=1), (HQ, HT * B), 0), jnp.concatenate(blocks, axis=0)
        )
        total[...] = part if g == 0 else total[...] + part
    first = core_ref[0] == 0
    for q in range(HK // 2):
        lower = total[:, q * E : (q + 1) * E]
        higher = total[:, (q + HK // 2) * E : (q + HK // 2 + 1) * E]
        rows = slice(q * HQ, (q + 1) * HQ)
        mine_ref[rows, :] = jnp.where(first, lower, higher)
        other_ref[rows, :] = jnp.where(first, higher, lower).astype(bf)


def share_kernel(x_ref, mine_ref, met_ref, own_ref, one_ref, two_ref, three_ref):
    part = own_ref.shape[0]
    for k, out in enumerate((own_ref, one_ref, two_ref, three_ref)):
        start = pl.multiple_of(lax.rem(x_ref[0] + k, 4) * part, part)
        chip = mine_ref[pl.ds(start, part), :] + met_ref[pl.ds(start, part), :].astype(f32)
        out[...] = chip.astype(out.dtype)


def cold_kernel(count_ref, rows_ref, returned_ref, table_ref, accum_ref, out_ref):
    lane = lax.broadcasted_iota(jnp.int32, (1, CAP), 1)
    flat = jnp.concatenate(
        [jnp.where(lane < count_ref[0, s], rows_ref[s : s + 1, :], -1) for s in range(NT)], axis=1
    )
    grad = dot(hit(flat, 0, (ROWS, SLOTS), 0), returned_ref[...])
    updated = accum_ref[...] + jnp.mean(grad * grad, axis=1, keepdims=True)
    out_ref[...] = table_ref[...].astype(f32) - grad / jnp.sqrt(updated)


def sds(shape, dtype):
    return jax.ShapeDtypeStruct(shape, dtype)


def pick(count, rows_t, table):
    return call(pick_kernel, sds((SLOTS, E), bf), [SM, VM, VM], [pltpu.VMEM((ROWS // 2, 2 * E), bf)], 2 * SLOTS * ROWS * E, 2000000, 62)(
        count, rows_t, table
    )


def hot_pool(ids, table, dense, one, two, three):
    return call(hot_kernel, (sds((BAGS, E), f32), sds((B, E), bf)), [VM] * 6, (), 2 * BAGS * HOT * E, 4000000)(
        ids, table, dense, one, two, three
    )


def cross(hot, bottom, arrived, bags, bags_t, grad, head, down, up):
    return call(
        cross_kernel,
        (sds((B, 1), f32), sds((HB, 2 * E), bf), sds((SLOTS, E), bf)),
        [VM] * 7 + [ANY] * 2,
        [
            pltpu.VMEM((F, R), bf),
            pltpu.VMEM((R, F), bf),
            pltpu.VMEM((HB, 2 * E), f32),
            pltpu.VMEM((B, F), bf),
            pltpu.SemaphoreType.DMA((2,)),
        ],
        4 * BAGS * SLOTS * E + 8 * B * F * R,
        14000000,
        60,
    )(hot, bottom, arrived, bags, bags_t, grad, head, down, up)


def hot_sum(core, bag_grad, ids, ids_t):
    return call(
        hot_grad_kernel,
        (sds((HOT // 2, E), f32), sds((HOT // 2, E), bf)),
        [SM] + [VM] * 3,
        [pltpu.VMEM((HQ, HK * E), f32)],
        2 * BAGS * HOT * E,
        3000000,
        32,
    )(core, bag_grad, ids, ids_t)


def shares(x, mine, met):
    part = HOT // 8
    return call(
        share_kernel,
        (sds((part, E), f32),) + (sds((part, E), bf),) * 3,
        [SM] + [VM] * 2,
        (),
        HOT * E,
        2000000,
    )(x, mine, met)


def cold_update(count, rows, returned, table, accum):
    return call(cold_kernel, sds((ROWS, E), f32), [SM] + [VM] * 4, (), 2 * ROWS * SLOTS * E, 2000000)(
        count, rows, returned, table, accum
    )


def a2a(v, axis, groups=None):
    return lax.all_to_all(v, axis, split_axis=0, concat_axis=0, tiled=True, axis_index_groups=groups)


def body(
    dense_input,
    hot_ids,
    logit_grad,
    hot_table,
    hot_accum,
    cold_table,
    cold_accum,
    send_rows,
    send_count,
    recv_bags,
    bottom_one,
    bottom_two,
    bottom_three,
    cross_down,
    cross_up,
    head_vector,
):
    n_dp = lax.axis_size("dp")
    n_xy = n_dp // 2
    n_y = n_xy // 4
    whole = [[(2 * k + c) * NT + z for k in range(n_xy) for z in range(NT)] for c in range(2)]
    slab = [g[n_y * NT * x : n_y * NT * (x + 1)] for g in whole for x in range(4)]
    twin = [(i, i ^ 1) for i in range(n_dp)]
    outgoing = pick(send_count, send_rows, cold_table)
    arrived = a2a(outgoing, "table")
    bags_t = recv_bags.T
    ids = jnp.pad(hot_ids, ((0, 0), (0, 128 - TABLES * LH)))
    hot, bottom = hot_pool(ids, hot_table, dense_input, bottom_one, bottom_two, bottom_three)
    core = lax.rem(lax.axis_index("dp"), 2)
    x_at = lax.div(lax.axis_index("dp"), 2 * n_y)
    half = HOT // 2
    logits, bag_grad, slot_grad = cross(
        hot, bottom, arrived, recv_bags, bags_t, logit_grad[:, None], head_vector[None, :], cross_down, cross_up
    )
    returned = a2a(slot_grad, "table")
    mine, other = hot_sum(core[None], bag_grad, hot_ids, hot_ids.T)
    met = lax.ppermute(other, "dp", twin)
    total, *parts = shares(x_at[None], mine, met)
    for k in range(1, 4):
        ahead = [(i, (i + 2 * n_y * k) % n_dp) for i in range(n_dp)]
        total = total + lax.ppermute(parts[k - 1], "dp", ahead).astype(f32)
    total, returned = lax.optimization_barrier((total.astype(bf), returned))
    share = half // (n_xy * NT)
    both = ("dp", "table")
    column = a2a(total, both, slab)
    new_cold = cold_update(send_count, send_rows, returned, cold_table, cold_accum[:, None])
    column, new_cold = lax.optimization_barrier((column, new_cold))
    grad = jnp.sum(column.reshape(n_y * NT, share, E).astype(f32), axis=0)
    first = core * half + (lax.div(lax.axis_index("dp"), 2) * NT + lax.axis_index("table")) * share
    accum = lax.dynamic_slice_in_dim(hot_accum, first, share, 0)
    step = grad / jnp.sqrt(accum + jnp.mean(grad * grad, axis=1))[:, None]
    step = step.astype(bf)
    steps = a2a(jnp.broadcast_to(step[None], (n_xy * NT, share, E)).reshape(half, E), both, whole)
    others = lax.ppermute(steps, "dp", twin)
    low = jnp.where(core == 0, steps, others)
    high = jnp.where(core == 0, others, steps)
    new_hot = hot_table.astype(f32) - jnp.concatenate([low, high], axis=0).astype(f32)
    return (logits[:, 0], new_hot, new_cold)


def solution(mesh):
    rows = P(("dp", "table"), None)
    flat = P(("dp", "table"))
    return jax.shard_map(
        body,
        mesh=mesh,
        in_specs=(rows, rows, flat, P(), P(), rows, flat, rows, rows, rows, P(), P(), P(), P(), P(), P()),
        out_specs=(flat, P(), rows),
        check_vma=False,
    )
```

```python
import jax
import jax.numpy as jnp
from jax import lax
from jax.experimental import pallas as pl
from jax.experimental.pallas import tpu as pltpu
from jax.sharding import PartitionSpec as P

E = 128
TABLES = 26
HALF = 13
LH = 2
HOT = 3072
B = 128
ROWS = 512
CAP = 256
NT = 12
SLOTS = NT * CAP
BAGS = B * TABLES
HB = B * HALF
R = 512
F = 3456
f32 = jnp.float32
bf = jnp.bfloat16
MIB = 1024 * 1024
VM = pl.BlockSpec(memory_space=pltpu.VMEM)
ANY = pl.BlockSpec(memory_space=pl.ANY)
SM = pl.BlockSpec(memory_space=pltpu.SMEM)


def dot(a, b):
    return jnp.dot(a, b, preferred_element_type=f32)


def dot_t(a, b):
    return lax.dot_general(a, b, (((1,), (1,)), ((), ())), preferred_element_type=f32)


def hit(idx, base, shape, axis):
    place = lax.broadcasted_iota(jnp.int32, shape, axis)
    return jnp.where(idx - base == place, 1.0, 0.0).astype(bf)


def call(kernel, outs, n_in_specs, scratch=(), flops=0, nbytes=0, mib=24):
    return pl.pallas_call(
        kernel,
        out_shape=outs,
        in_specs=n_in_specs,
        out_specs=jax.tree.map(lambda _: VM, outs),
        scratch_shapes=list(scratch),
        compiler_params=pltpu.CompilerParams(vmem_limit_bytes=mib * MIB),
        cost_estimate=pl.CostEstimate(flops=flops, bytes_accessed=nbytes, transcendentals=0),
    )


def split_bag(bag):
    sample = (bag * 2521) >> 16
    table = bag - sample * TABLES
    upper = table >= HALF
    return upper, jnp.where(upper, table - HALF, table) * B + sample


def pick_kernel(count_ref, rows_ref, table_ref, out_ref, wide):
    rows_t = rows_ref[...].T
    wide[:, :E] = table_ref[: ROWS // 2, :]
    wide[:, E:] = table_ref[ROWS // 2 :, :]
    slot = lax.broadcasted_iota(jnp.int32, (CAP, 1), 0)
    for s in range(NT):
        row = rows_t[:, s : s + 1]
        row = jnp.where(slot < count_ref[0, s], row, -1)
        upper = row >= ROWS // 2
        low = jnp.where(upper, row - ROWS // 2, row)
        both = dot(hit(low, 0, (CAP, ROWS // 2), 1), wide[...])
        out_ref[s * CAP : (s + 1) * CAP, :] = jnp.where(upper, both[:, E:], both[:, :E]).astype(bf)


def hot_kernel(ids_ref, table_ref, dense_ref, one_ref, two_ref, three_ref, out_ref, bottom_ref):
    first = jnp.maximum(dot(dense_ref[...], one_ref[...]), 0.0).astype(bf)
    second = jnp.maximum(dot(first, two_ref[...]), 0.0).astype(bf)
    bottom_ref[...] = jnp.maximum(dot(second, three_ref[...]), 0.0).astype(bf)

    def pair(j, _):
        ids = pltpu.roll(ids_ref[...], lax.rem(128 - 4 * j, 128), 1)
        left = jnp.concatenate([ids[:, 0:1], ids[:, 2:3]], axis=0)
        right = jnp.concatenate([ids[:, 1:2], ids[:, 3:4]], axis=0)
        count = hit(left, 0, (2 * B, HOT), 1) + hit(right, 0, (2 * B, HOT), 1)
        out_ref[pl.ds(pl.multiple_of(j * 2 * B, 2 * B), 2 * B), :] = dot(count, table_ref[...])
        return 0

    lax.fori_loop(0, HALF, pair, 0)


HK = 4
HQ = HOT // HK
HT = 26
SG = 4


def mark(idx, shape, axis):
    place = lax.broadcasted_iota(jnp.int16, shape, axis)
    return jnp.where(idx.astype(jnp.int16) == place, jnp.ones(shape, bf), jnp.zeros(shape, bf))


def spot(t):
    r = (t % HALF) * B
    c = (t // HALF) * E
    return slice(r, r + B), slice(c, c + E)


def cross_kernel(
    hot_ref,
    bottom_ref,
    arrived_ref,
    bags_ref,
    bags_t_ref,
    grad_ref,
    head_ref,
    down_hbm,
    up_hbm,
    logits_ref,
    bag_grad_ref,
    slot_ref,
    down,
    up,
    cold,
    x0,
    sems,
):
    copy_down = pltpu.make_async_copy(down_hbm, down, sems.at[0])
    copy_up = pltpu.make_async_copy(up_hbm, up, sems.at[1])
    copy_down.start()
    copy_up.start()
    zero = jnp.zeros((CAP, E), bf)
    _, place = split_bag(bags_ref[...])
    for g in range(2):
        owners = range(6 * g, 6 * g + 6)
        wide = []
        for s in owners:
            upper, _ = split_bag(bags_t_ref[:, s : s + 1])
            block = arrived_ref[s * CAP : (s + 1) * CAP, :]
            wide.append(jnp.concatenate([jnp.where(upper, zero, block), jnp.where(upper, block, zero)], axis=1))
        flat = jnp.concatenate([place[s : s + 1, :] for s in owners], axis=1)
        part = dot(mark(flat, (HB, 6 * CAP), 0), jnp.concatenate(wide, axis=0))
        cold[...] = part if g == 0 else cold[...] + part
    x0[:, :E] = bottom_ref[...]
    for t in range(TABLES):
        r, c = spot(t)
        x0[:, E * (t + 1) : E * (t + 2)] = (hot_ref[t * B : (t + 1) * B, :] + cold[r, c]).astype(bf)
    upstream = grad_ref[...]
    copy_down.wait()
    copy_up.wait()
    low = dot(x0[...], down[...]).astype(bf)
    low_grad = dot_t((upstream * head_ref[...] * x0[...].astype(f32)).astype(bf), up[...]).astype(bf)
    logit = jnp.zeros((B, E), f32)
    for k in range(0, TABLES + 1, 3):
        cols = slice(E * k, E * (k + 3))
        head = head_ref[:, cols]
        gated = dot(low, up[:, cols]) + 1.0
        part = x0[:, cols].astype(f32) * gated * head
        logit = logit + part[:, :E] + part[:, E : 2 * E] + part[:, 2 * E :]
        back = upstream * head * gated + dot_t(low_grad, down[cols, :])
        for i in range(3):
            if k + i > 0:
                r, c = spot(k + i - 1)
                bag_grad_ref[r, c] = back[:, E * i : E * (i + 1)].astype(bf)
    logits_ref[...] = jnp.sum(logit, axis=1, keepdims=True)
    for g in range(0, NT, SG):
        halves, marks = [], []
        for s in range(g, g + SG):
            upper, place = split_bag(bags_t_ref[:, s : s + 1])
            halves.append(upper)
            marks.append(hit(place, 0, (CAP, HB), 1))
        both = dot(jnp.concatenate(marks, axis=0), bag_grad_ref[...])
        upper = jnp.concatenate(halves, axis=0)
        slot_ref[g * CAP : (g + SG) * CAP, :] = jnp.where(upper, both[:, E:], both[:, :E]).astype(bf)


def hot_grad_kernel(core_ref, bag_grad_ref, ids_ref, ids_t_ref, mine_ref, other_ref, total):
    none = jnp.zeros((B, E), bf)
    low_ids = lax.rem(ids_t_ref[...], HQ)
    for g in range(TABLES * LH // HT):
        places, blocks = [], []
        for i in range(HT):
            n = g * HT + i
            r, c = spot(n // LH)
            block = bag_grad_ref[r, c]
            col = ids_ref[:, n : n + 1]
            blocks.append(
                jnp.concatenate(
                    [jnp.where((col >= q * HQ) & (col < (q + 1) * HQ), block, none) for q in range(HK)], axis=1
                )
            )
            places.append(low_ids[n : n + 1, :])
        part = dot(
            mark(jnp.concatenate(places, axis=1), (HQ, HT * B), 0), jnp.concatenate(blocks, axis=0)
        )
        total[...] = part if g == 0 else total[...] + part
    first = core_ref[0] == 0
    for q in range(HK // 2):
        lower = total[:, q * E : (q + 1) * E]
        higher = total[:, (q + HK // 2) * E : (q + HK // 2 + 1) * E]
        rows = slice(q * HQ, (q + 1) * HQ)
        mine_ref[rows, :] = jnp.where(first, lower, higher)
        other_ref[rows, :] = jnp.where(first, higher, lower).astype(bf)


def share_kernel(x_ref, mine_ref, met_ref, own_ref, one_ref, two_ref, three_ref):
    part = own_ref.shape[0]
    for k, out in enumerate((own_ref, one_ref, two_ref, three_ref)):
        start = pl.multiple_of(lax.rem(x_ref[0] + k, 4) * part, part)
        chip = mine_ref[pl.ds(start, part), :] + met_ref[pl.ds(start, part), :].astype(f32)
        out[...] = chip.astype(out.dtype)


def cold_kernel(count_ref, rows_ref, returned_ref, table_ref, accum_ref, out_ref):
    lane = lax.broadcasted_iota(jnp.int32, (1, CAP), 1)
    flat = jnp.concatenate(
        [jnp.where(lane < count_ref[0, s], rows_ref[s : s + 1, :], -1) for s in range(NT)], axis=1
    )
    grad = dot(hit(flat, 0, (ROWS, SLOTS), 0), returned_ref[...])
    updated = accum_ref[...] + jnp.mean(grad * grad, axis=1, keepdims=True)
    out_ref[...] = table_ref[...].astype(f32) - grad / jnp.sqrt(updated)


def sds(shape, dtype):
    return jax.ShapeDtypeStruct(shape, dtype)


def pick(count, rows_t, table):
    return call(pick_kernel, sds((SLOTS, E), bf), [SM, VM, VM], [pltpu.VMEM((ROWS // 2, 2 * E), bf)], 2 * SLOTS * ROWS * E, 2000000, 62)(
        count, rows_t, table
    )


def hot_pool(ids, table, dense, one, two, three):
    return call(hot_kernel, (sds((BAGS, E), f32), sds((B, E), bf)), [VM] * 6, (), 2 * BAGS * HOT * E, 4000000)(
        ids, table, dense, one, two, three
    )


def cross(hot, bottom, arrived, bags, bags_t, grad, head, down, up):
    return call(
        cross_kernel,
        (sds((B, 1), f32), sds((HB, 2 * E), bf), sds((SLOTS, E), bf)),
        [VM] * 7 + [ANY] * 2,
        [
            pltpu.VMEM((F, R), bf),
            pltpu.VMEM((R, F), bf),
            pltpu.VMEM((HB, 2 * E), f32),
            pltpu.VMEM((B, F), bf),
            pltpu.SemaphoreType.DMA((2,)),
        ],
        4 * BAGS * SLOTS * E + 8 * B * F * R,
        14000000,
        60,
    )(hot, bottom, arrived, bags, bags_t, grad, head, down, up)


def hot_sum(core, bag_grad, ids, ids_t):
    return call(
        hot_grad_kernel,
        (sds((HOT // 2, E), f32), sds((HOT // 2, E), bf)),
        [SM] + [VM] * 3,
        [pltpu.VMEM((HQ, HK * E), f32)],
        2 * BAGS * HOT * E,
        3000000,
        32,
    )(core, bag_grad, ids, ids_t)


def shares(x, mine, met):
    part = HOT // 8
    return call(
        share_kernel,
        (sds((part, E), f32),) + (sds((part, E), bf),) * 3,
        [SM] + [VM] * 2,
        (),
        HOT * E,
        2000000,
    )(x, mine, met)


def cold_update(count, rows, returned, table, accum):
    return call(cold_kernel, sds((ROWS, E), f32), [SM] + [VM] * 4, (), 2 * ROWS * SLOTS * E, 2000000)(
        count, rows, returned, table, accum
    )


def a2a(v, axis, groups=None):
    return lax.all_to_all(v, axis, split_axis=0, concat_axis=0, tiled=True, axis_index_groups=groups)


def body(
    dense_input,
    hot_ids,
    logit_grad,
    hot_table,
    hot_accum,
    cold_table,
    cold_accum,
    send_rows,
    send_count,
    recv_bags,
    bottom_one,
    bottom_two,
    bottom_three,
    cross_down,
    cross_up,
    head_vector,
):
    n_dp = lax.axis_size("dp")
    n_xy = n_dp // 2
    n_y = n_xy // 4
    xy_groups = [[2 * k + c for k in range(n_xy)] for c in range(2)]
    y_groups = [[2 * n_y * x + 2 * y + c for y in range(n_y)] for x in range(4) for c in range(2)]
    twin = [(i, i ^ 1) for i in range(n_dp)]
    outgoing = pick(send_count, send_rows, cold_table)
    arrived = a2a(outgoing, "table")
    bags_t = recv_bags.T
    ids = jnp.pad(hot_ids, ((0, 0), (0, 128 - TABLES * LH)))
    hot, bottom = hot_pool(ids, hot_table, dense_input, bottom_one, bottom_two, bottom_three)
    core = lax.rem(lax.axis_index("dp"), 2)
    x_at = lax.div(lax.axis_index("dp"), 2 * n_y)
    half = HOT // 2
    logits, bag_grad, slot_grad = cross(
        hot, bottom, arrived, recv_bags, bags_t, logit_grad[:, None], head_vector[None, :], cross_down, cross_up
    )
    returned = a2a(slot_grad, "table")
    mine, other = hot_sum(core[None], bag_grad, hot_ids, hot_ids.T)
    met = lax.ppermute(other, "dp", twin)
    total, *parts = shares(x_at[None], mine, met)
    for k in range(1, 4):
        ahead = [(i, (i + 2 * n_y * k) % n_dp) for i in range(n_dp)]
        total = total + lax.ppermute(parts[k - 1], "dp", ahead).astype(f32)
    total, returned = lax.optimization_barrier((total.astype(bf), returned))
    share = half // n_xy
    line = a2a(total, "dp", y_groups)
    plane = jnp.sum(line.reshape(n_y, share, E).astype(f32), axis=0).astype(bf)
    column = a2a(jnp.broadcast_to(plane[None], (NT, share, E)).reshape(NT * share, E), "table")
    new_cold = cold_update(send_count, send_rows, returned, cold_table, cold_accum[:, None])
    column, new_cold = lax.optimization_barrier((column, new_cold))
    grad = jnp.sum(column.reshape(NT, share, E).astype(f32), axis=0)
    first = core * half + lax.div(lax.axis_index("dp"), 2) * share
    accum = lax.dynamic_slice_in_dim(hot_accum, first, share, 0)
    step = grad / jnp.sqrt(accum + jnp.mean(grad * grad, axis=1))[:, None]
    step = step.astype(bf)
    steps = a2a(jnp.broadcast_to(step[None], (n_xy, share, E)).reshape(half, E), "dp", xy_groups)
    others = lax.ppermute(steps, "dp", twin)
    low = jnp.where(core == 0, steps, others)
    high = jnp.where(core == 0, others, steps)
    new_hot = hot_table.astype(f32) - jnp.concatenate([low, high], axis=0).astype(f32)
    return (logits[:, 0], new_hot, new_cold)


def solution(mesh):
    rows = P(("dp", "table"), None)
    flat = P(("dp", "table"))
    return jax.shard_map(
        body,
        mesh=mesh,
        in_specs=(rows, rows, flat, P(), P(), rows, flat, rows, rows, rows, P(), P(), P(), P(), P(), P()),
        out_specs=(flat, P(), rows),
        check_vma=False,
    )
```
